256 devices in a mesh: wa: 8 (over z_lo, x), ha: 32 (over y, z_hi, core).
Axes of the slice: x: 4, y: 4, z: 8 (z_hi: 4, z_lo: 2; z = z_hi * 2 + z_lo), core: 2. Of those that a mesh axis runs over, the one named last changes fastest.
Arguments:
- tokens: float32 [256, 5376], P('ha', 'wa'), may hold values from -6 to 6
- grad_out: float32 [256, 5376], P('ha', 'wa'), may hold values from -1.5 to 1.5
- gate_weight: float32 [5376, 10752], P('wa', 'ha'), may hold values from -0.078125 to 0.078125
- up_weight: float32 [5376, 10752], P('wa', 'ha'), may hold values from -0.078125 to 0.078125
- down_weight: float32 [10752, 5376], P('ha', 'wa'), may hold values from -0.0625 to 0.0625
Outputs:
- grad_tokens: float32 [256, 5376], P('ha', 'wa')
- grad_gate: float32 [5376, 10752], P('wa', 'ha')
- grad_up: float32 [5376, 10752], P('wa', 'ha')
- grad_down: float32 [10752, 5376], P('ha', 'wa')
The draws below stay inside these ranges and needn't reach their ends.
All inputs are finite; a program needn't handle non-finite values.
Results may differ from the reference program's by a relative error of at most 0.00018.
Values sent between devices are 32-bit elements; how exact they have to be, the bound alone decides.
A program may use at most 64 MiB of HBM per device.

```python
import jax
import jax.numpy as jnp
from jax import lax

D = 5376
FF = 10752
TOKENS = 256


def levels(stream_key, extent, shards, least, top_value):
    loudness, own = 1.0, jax.random.fold_in(stream_key, 6)
    for position, shards_of in shards:
        steps = jnp.exp(jax.random.uniform(jax.random.fold_in(own, position), (shards_of,), jnp.float32, least / len(shards), top_value / len(shards)))
        loudness = loudness * jnp.repeat(steps, extent[position] // shards_of).reshape([-1 if axis == position else 1 for axis in range(len(extent))])
    return loudness


def gaussian(key, extent, width, most, shards=(), dtype=jnp.bfloat16):
    gain = levels(key, extent, shards, -0.22, 0.18) if shards else 1.0
    entries = jax.random.normal(key, extent, jnp.float32) * width * gain
    return jnp.minimum(jnp.maximum(entries, -most), most).astype(dtype)


def setup_inputs(seed: int = 0) -> dict:
    key_of = jax.random.split(jax.random.key(seed), 6)
    return {
        "tokens": gaussian(key_of[0], (TOKENS, D), 1.0, 6.0, ((0, 32), (1, 8)), jnp.float32),
        "grad_out": gaussian(key_of[1], (TOKENS, D), 0.25, 1.5, ((0, 32), (1, 8)), jnp.float32),
        "gate_weight": gaussian(key_of[2], (D, FF), D ** -0.5, 0.078125, ((0, 8), (1, 32)), jnp.float32),
        "up_weight": gaussian(key_of[3], (D, FF), D ** -0.5, 0.078125, ((0, 8), (1, 32)), jnp.float32),
        "down_weight": gaussian(key_of[4], (FF, D), FF ** -0.5, 0.0625, ((0, 32), (1, 8)), jnp.float32),
    }


def matmul(left, right):
    return jnp.dot(left, right, preferred_element_type=jnp.float32, precision=lax.Precision.HIGHEST)


def reference(tokens, grad_out, gate_weight, up_weight, down_weight):
    gate = matmul(tokens, gate_weight)
    up = matmul(tokens, up_weight)
    grad_hidden = matmul(grad_out, down_weight.T)
    sig = 1.0 / (1.0 + jnp.exp(-gate))
    hidden = gate * sig * up
    grad_up_act = grad_hidden * gate * sig
    grad_gate_act = grad_hidden * up * sig * (1.0 + gate * (1.0 - sig))
    grad_down = matmul(hidden.T, grad_out)
    grad_gate = matmul(tokens.T, grad_gate_act)
    grad_up = matmul(tokens.T, grad_up_act)
    grad_tokens = matmul(grad_gate_act, gate_weight.T) + matmul(grad_up_act, up_weight.T)
    return grad_tokens, grad_gate, grad_up, grad_down
```

```python
import jax
import jax.numpy as jnp
from jax import lax
from jax.experimental import pallas as pl
from jax.experimental.pallas import tpu as pltpu
from jax.sharding import PartitionSpec as P

MESH = pl.DeviceIdType.MESH
F32, BF16 = jnp.float32, jnp.bfloat16
DL, FL = 672, 336
DP, FP = 768, 384
XW, AW = 1408, 1024
STEPS = (0, 1, 3, 2)


def split(v):
    hi = v.astype(BF16)
    return hi, (v - hi.astype(F32)).astype(BF16)


def dot(a, b, ad, bd):
    return lax.dot_general(a, b, (((ad,), (bd,)), ((), ())), preferred_element_type=F32)


def pack3(a, b, c):
    rows = a.shape[0]
    return jnp.concatenate([a[:, :FL], b[:, :FL], c[:, :FL], jnp.zeros((rows, AW - 3 * FL), F32)], axis=1)


def unpack3(p):
    pad = jnp.zeros((p.shape[0], FP - FL), F32)
    return [jnp.concatenate([p[:, i * FL : (i + 1) * FL], pad], axis=1) for i in range(3)]


def derivs(gate, up, grad_hidden):
    sig = 1.0 / (1.0 + jnp.exp(-gate))
    hidden = gate * sig * up
    grad_up_act = grad_hidden * gate * sig
    grad_gate_act = grad_hidden * up * sig * (1.0 + gate * (1.0 - sig))
    return grad_gate_act, grad_up_act, hidden


def kernel(
    tok, gro, wg_hbm, wu_hbm, wd_hbm,
    o_tok, o_g, o_u, o_d,
    wg, wu, wd, wgu_h, wgu_l, wd_h, wd_l,
    x, xt_h, xt_l, xg_h, xg_l,
    part, part_in, acts, a_h, a_l,
    gb, gb_in, q, q_in, r, r_in, og, ou, od,
    w_sem, az_s, az_r, ay_s, ay_r, as_s, as_r, fs_s, fs_r,
    b_s, b_r, c_s, c_r, d1_s, d1_r, d2_s, d2_r, d3_s, d3_r, o_sem,
):
    wa, ha = lax.axis_index("wa"), lax.axis_index("ha")
    y, zh, c = ha // 8, (ha // 2) % 4, ha % 2

    def dev(w, yy, zz, cc):
        return (w, yy * 8 + zz * 2 + cc)

    sibling = dev(wa, y, zh, 1 - c)
    z_peers = [dev(wa, y, (zh + i) % 4, c) for i in (1, 2, 3)]
    y_peers = [dev(wa, (y + s) % 4, zh, c) for s in STEPS[1:]]
    w_peers = [dev((wa + i) % 8, y, zh, c) for i in range(1, 8)]

    loads = [
        pltpu.make_async_copy(wg_hbm, wg, w_sem.at[0]),
        pltpu.make_async_copy(wu_hbm, wu, w_sem.at[1]),
        pltpu.make_async_copy(wd_hbm, wd, w_sem.at[2]),
    ]
    for cp in loads:
        cp.start()

    barrier = pltpu.get_barrier_semaphore()
    for d in [sibling, *z_peers, *y_peers, *w_peers]:
        pl.semaphore_signal(barrier, inc=1, device_id=d, device_id_type=MESH)
    t, g = tok[...], gro[...]
    x[y, c, zh] = jnp.concatenate([t[:, :640], g[:, :640], t[:, 640:], g[:, 640:], jnp.zeros((8, 64), F32)], axis=1)
    pl.semaphore_wait(barrier, 14)

    sends = []

    def send(src, dst, ss, rs, d):
        cp = pltpu.make_async_remote_copy(src_ref=src, dst_ref=dst, send_sem=ss, recv_sem=rs, device_id=d, device_id_type=MESH)
        cp.start()
        sends.append(cp)

    def arrived(ref, sem):
        pltpu.make_async_copy(ref, ref, sem).wait()

    own = x.at[y, c, zh]
    for i in range(3):
        send(own, own, az_s.at[i], az_r.at[i], z_peers[i])
    for k in range(3):
        send(own, own, ay_s.at[0, k], ay_r.at[k, 0], y_peers[k])
    send(own, own, as_s.at[0], as_r.at[0], sibling)

    wgu_h[DL:, :] = jnp.zeros((DP - DL, DP), BF16)
    wgu_l[DL:, :] = jnp.zeros((DP - DL, DP), BF16)
    wd_h[FL:, :] = jnp.zeros((FP - FL, DP), BF16)
    wd_l[FL:, :] = jnp.zeros((FP - FL, DP), BF16)
    loads[0].wait()
    loads[1].wait()

    @pl.loop(0, 7)
    def _(i):
        rows = pl.ds(pl.multiple_of(i * 96, 96), 96)
        pad = jnp.zeros((96, FP - FL), F32)
        hi, lo = split(jnp.concatenate([wg[rows, :], pad], axis=1))
        wgu_h[rows, :FP], wgu_l[rows, :FP] = hi, lo
        hi, lo = split(jnp.concatenate([wu[rows, :], pad], axis=1))
        wgu_h[rows, FP:], wgu_l[rows, FP:] = hi, lo

    loads[2].wait()

    @pl.loop(0, 7)
    def _(i):
        rows = pl.ds(pl.multiple_of(i * 48, 48), 48)
        hi, lo = split(jnp.concatenate([wd[rows, :], jnp.zeros((48, DP - DL), F32)], axis=1))
        wd_h[rows, :], wd_l[rows, :] = hi, lo

    for i in range(3):
        block = x.at[y, c, (zh - i - 1 + 4) % 4]
        arrived(block, az_r.at[i])
        for k in range(3):
            send(block, block, ay_s.at[i + 1, k], ay_r.at[k, i + 1], y_peers[k])
        send(block, block, as_s.at[i + 1], as_r.at[i + 1], sibling)

    def source_y(k):
        return (y + 4 - STEPS[k]) % 4

    def forward(k):
        yy = source_y(k)
        for i in range(4):
            arrived(x.at[yy, c, (zh - i + 4) % 4], ay_r.at[k - 1, i])
        send(x.at[yy, c], x.at[yy, c], fs_s.at[k - 1], fs_r.at[k - 1], sibling)

    lane = lax.broadcasted_iota(jnp.int32, (64, 128), 1)

    def project(k):
        yy = source_y(k)
        if k == 0:
            for i in range(4):
                arrived(x.at[yy, 1 - c, (zh - i + 4) % 4], as_r.at[i])
        else:
            arrived(x.at[yy, 1 - c], fs_r.at[k - 1])
        rows = pl.ds(pl.multiple_of(yy * 64, 64), 64)
        v = x[yy].reshape(64, XW)
        mixed = v[:, 1280:]
        th, tl = split(jnp.concatenate([v[:, :640], jnp.where(lane < 32, mixed, 0.0)], axis=1))
        gh, gl = split(jnp.concatenate([v[:, 640:1280], jnp.where(lane < 32, pltpu.roll(mixed, 96, 1), 0.0)], axis=1))
        xt_h[rows, :], xt_l[rows, :] = th, tl
        xg_h[rows, :], xg_l[rows, :] = gh, gl
        both = jnp.concatenate([th, tl], axis=0)
        gu = dot(both, wgu_h[...], 1, 0)
        gu = gu[:64] + gu[64:] + dot(th, wgu_l[...], 1, 0)
        both = jnp.concatenate([gh, gl], axis=0)
        hid = dot(both, wd_h[...], 1, 1)
        hid = hid[:64] + hid[64:] + dot(gh, wd_l[...], 1, 1)
        part[k] = pack3(gu[:, :FP], gu[:, FP:], hid).reshape(8, 8, AW)
        for i in range(7):
            send(part.at[k, (wa + i + 1) % 8], part_in.at[k, i], b_s.at[k, i], b_r.at[k, i], w_peers[i])

    def activate(k):
        yy = source_y(k)
        total = part[k, wa]
        for i in range(7):
            arrived(part_in.at[k, i], b_r.at[k, i])
            total = total + part_in[k, i]
        gate, up, gh = unpack3(total)
        acts[yy, wa] = pack3(*derivs(gate, up, gh))
        mine = acts.at[yy, wa]
        for i in range(7):
            send(mine, mine, c_s.at[k, i], c_r.at[k, i], w_peers[i])

    def back(k):
        yy = source_y(k)
        for i in range(7):
            arrived(acts.at[yy, (wa - i - 1 + 8) % 8], c_r.at[k, i])
        rows = pl.ds(pl.multiple_of(yy * 64, 64), 64)
        gga, gua, hid = unpack3(acts[yy].reshape(64, AW))
        ah, al = split(jnp.concatenate([gga, gua], axis=1))
        hh, hl = split(hid)
        a_h[rows, :DP], a_l[rows, :DP] = ah, al
        a_h[rows, DP:], a_l[rows, DP:] = hh, hl
        both = jnp.concatenate([ah, al], axis=0)
        gt = dot(both, wgu_h[...], 1, 1)
        gt = gt[:64] + gt[64:] + dot(ah, wgu_l[...], 1, 1)
        gb[k] = gt.reshape(2, 4, 8, DP)
        send(gb.at[k, 1 - c], gb_in.at[k], d1_s.at[k], d1_r.at[k], sibling)

    def home(k):
        arrived(gb_in.at[k], d1_r.at[k])
        q[k] = gb[k, c] + gb_in[k]
        if k:
            yy = source_y(k)
            send(q.at[k], q_in.at[k - 1], d2_s.at[k - 1], d2_r.at[k - 1], dev(wa, yy, zh, c))

    project(0)
    forward(1)
    forward(2)
    project(1)
    activate(0)
    project(2)
    forward(3)
    activate(1)
    project(3)
    back(0)
    activate(2)
    back(1)
    home(0)
    activate(3)
    back(2)
    home(1)
    back(3)
    home(2)

    stores = []

    def store(src, dst, i):
        cp = pltpu.make_async_copy(src, dst, o_sem.at[i])
        cp.start()
        stores.append(cp)

    def grad(lh, ll, rh, rl):
        return dot(lh, rh, 0, 0) + dot(lh, rl, 0, 0) + dot(ll, rh, 0, 0)

    home(3)
    gg = grad(xt_h[...], xt_l[...], a_h[:, :FP], a_l[:, :FP])
    og[...] = gg[:DL, :FL]
    store(og, o_g, 0)

    total = q[0]
    for k in range(3):
        arrived(q_in.at[k], d2_r.at[k])
        total = total + q_in[k]
    r[...] = total
    for i in range(3):
        send(r.at[(zh + i + 1) % 4], r_in.at[i], d3_s.at[i], d3_r.at[i], z_peers[i])

    gg = grad(xt_h[...], xt_l[...], a_h[:, FP:DP], a_l[:, FP:DP])
    ou[...] = gg[:DL, :FL]
    store(ou, o_u, 1)
    gg = grad(a_h[:, DP:], a_l[:, DP:], xg_h[...], xg_l[...])
    od[...] = gg[:FL, :DL]
    store(od, o_d, 2)

    total = r[zh]
    for i in range(3):
        arrived(r_in.at[i], d3_r.at[i])
        total = total + r_in[i]
    o_tok[...] = total[:, :DL]
    for cp in sends:
        cp.wait_send()
    for cp in stores:
        cp.wait()


def per_device(tokens, grad_out, gate_weight, up_weight, down_weight):
    vm, anym = pl.BlockSpec(memory_space=pltpu.VMEM), pl.BlockSpec(memory_space=pltpu.MemorySpace.HBM)
    dma = pltpu.SemaphoreType.DMA
    v = pltpu.VMEM
    return pl.pallas_call(
        kernel,
        out_shape=(
            jax.ShapeDtypeStruct((8, DL), F32),
            jax.ShapeDtypeStruct((DL, FL), F32),
            jax.ShapeDtypeStruct((DL, FL), F32),
            jax.ShapeDtypeStruct((FL, DL), F32),
        ),
        in_specs=[vm, vm, anym, anym, anym],
        out_specs=(vm, anym, anym, anym),
        scratch_shapes=[
            v((DL, FL), F32), v((DL, FL), F32), v((FL, DL), F32),
            v((DP, DP), BF16), v((DP, DP), BF16), v((FP, DP), BF16), v((FP, DP), BF16),
            v((4, 2, 4, 8, XW), F32),
            v((256, DP), BF16), v((256, DP), BF16), v((256, DP), BF16), v((256, DP), BF16),
            v((4, 8, 8, AW), F32), v((4, 7, 8, AW), F32), v((4, 8, 8, AW), F32),
            v((256, DP + FP), BF16), v((256, DP + FP), BF16),
            v((4, 2, 4, 8, DP), F32), v((4, 4, 8, DP), F32), v((4, 4, 8, DP), F32), v((3, 4, 8, DP), F32),
            v((4, 8, DP), F32), v((3, 8, DP), F32),
            v((DL, FL), F32), v((DL, FL), F32), v((FL, DL), F32),
            dma((3,)), dma((3,)), dma((3,)), dma((4, 3)), dma((3, 4)), dma((4,)), dma((4,)), dma((3,)), dma((3,)),
            dma((4, 7)), dma((4, 7)), dma((4, 7)), dma((4, 7)),
            dma((4,)), dma((4,)), dma((3,)), dma((3,)), dma((3,)), dma((3,)), dma((3,)),
        ],
        compiler_params=pltpu.CompilerParams(collective_id=0, has_side_effects=True, vmem_limit_bytes=40 * 2**20),
        name="feed_forward_backward",
    )(tokens, grad_out, gate_weight, up_weight, down_weight)


def solution(mesh):
    placed = (P("ha", "wa"), P("ha", "wa"), P("wa", "ha"), P("wa", "ha"), P("ha", "wa"))
    return jax.shard_map(
        per_device,
        mesh=mesh,
        in_specs=placed,
        out_specs=(P("ha", "wa"), P("wa", "ha"), P("wa", "ha"), P("ha", "wa")),
        check_vma=False,
    )
```

```python
import jax
import jax.numpy as jnp
from jax import lax
from jax.experimental import pallas as pl
from jax.experimental.pallas import tpu as pltpu
from jax.sharding import PartitionSpec as P

MESH = pl.DeviceIdType.MESH
F32, BF16 = jnp.float32, jnp.bfloat16
DL, FL = 672, 336
DP, FP = 768, 384
XW, AW = 1408, 1024
STEPS = (0, 1, 2, 3)


def split(v):
    hi = v.astype(BF16)
    return hi, (v - hi.astype(F32)).astype(BF16)


def dot(a, b, ad, bd):
    return lax.dot_general(a, b, (((ad,), (bd,)), ((), ())), preferred_element_type=F32)


def pack3(a, b, c):
    rows = a.shape[0]
    return jnp.concatenate([a[:, :FL], b[:, :FL], c[:, :FL], jnp.zeros((rows, AW - 3 * FL), F32)], axis=1)


def unpack3(p):
    pad = jnp.zeros((p.shape[0], FP - FL), F32)
    return [jnp.concatenate([p[:, i * FL : (i + 1) * FL], pad], axis=1) for i in range(3)]


def derivs(gate, up, grad_hidden):
    sig = 1.0 / (1.0 + jnp.exp(-gate))
    hidden = gate * sig * up
    grad_up_act = grad_hidden * gate * sig
    grad_gate_act = grad_hidden * up * sig * (1.0 + gate * (1.0 - sig))
    return grad_gate_act, grad_up_act, hidden


def kernel(
    tok, gro, wg_hbm, wu_hbm, wd_hbm,
    o_tok, o_g, o_u, o_d,
    wg, wu, wd, wgu_h, wgu_l, wd_h, wd_l,
    x, xt_h, xt_l, xg_h, xg_l,
    part, part_in, acts, a_h, a_l,
    gb, gb_in, q, q_in, r, r_in,
    w_sem, az_s, az_r, ay_s, ay_r, as_s, as_r,
    b_s, b_r, c_s, c_r, d1_s, d1_r, d2_s, d2_r, d3_s, d3_r,
):
    wa, ha = lax.axis_index("wa"), lax.axis_index("ha")
    y, zh, c = ha // 8, (ha // 2) % 4, ha % 2

    def dev(w, yy, zz, cc):
        return (w, yy * 8 + zz * 2 + cc)

    sibling = dev(wa, y, zh, 1 - c)
    z_peers = [dev(wa, y, (zh + i) % 4, c) for i in (1, 2, 3)]
    y_peers = [dev(wa, (y + s) % 4, zh, c) for s in STEPS[1:]]
    w_peers = [dev((wa + i) % 8, y, zh, c) for i in range(1, 8)]

    loads = [
        pltpu.make_async_copy(wg_hbm, wg, w_sem.at[0]),
        pltpu.make_async_copy(wu_hbm, wu, w_sem.at[1]),
        pltpu.make_async_copy(wd_hbm, wd, w_sem.at[2]),
    ]
    for cp in loads:
        cp.start()

    barrier = pltpu.get_barrier_semaphore()
    for d in [sibling, *z_peers, *y_peers, *w_peers]:
        pl.semaphore_signal(barrier, inc=1, device_id=d, device_id_type=MESH)
    t, g = tok[...], gro[...]
    x[zh, c, y] = jnp.concatenate([t[:, :640], g[:, :640], t[:, 640:], g[:, 640:], jnp.zeros((8, 64), F32)], axis=1)
    pl.semaphore_wait(barrier, 14)

    sends = []

    def send(src, dst, ss, rs, d):
        cp = pltpu.make_async_remote_copy(src_ref=src, dst_ref=dst, send_sem=ss, recv_sem=rs, device_id=d, device_id_type=MESH)
        cp.start()
        sends.append(cp)

    def arrived(ref, sem):
        pltpu.make_async_copy(ref, ref, sem).wait()

    own = x.at[zh, c, y]
    for i in (0, 2, 1):
        send(own, own, ay_s.at[0, i], ay_r.at[0, i], y_peers[i])
    for i in (0, 2, 1):
        send(own, own, az_s.at[i], az_r.at[i], z_peers[i])

    wgu_h[DL:, :] = jnp.zeros((DP - DL, DP), BF16)
    wgu_l[DL:, :] = jnp.zeros((DP - DL, DP), BF16)
    wd_h[FL:, :] = jnp.zeros((FP - FL, DP), BF16)
    wd_l[FL:, :] = jnp.zeros((FP - FL, DP), BF16)
    loads[0].wait()
    loads[1].wait()

    @pl.loop(0, 7)
    def _(i):
        rows = pl.ds(pl.multiple_of(i * 96, 96), 96)
        pad = jnp.zeros((96, FP - FL), F32)
        hi, lo = split(jnp.concatenate([wg[rows, :], pad], axis=1))
        wgu_h[rows, :FP], wgu_l[rows, :FP] = hi, lo
        hi, lo = split(jnp.concatenate([wu[rows, :], pad], axis=1))
        wgu_h[rows, FP:], wgu_l[rows, FP:] = hi, lo

    loads[2].wait()

    @pl.loop(0, 7)
    def _(i):
        rows = pl.ds(pl.multiple_of(i * 48, 48), 48)
        hi, lo = split(jnp.concatenate([wd[rows, :], jnp.zeros((48, DP - DL), F32)], axis=1))
        wd_h[rows, :], wd_l[rows, :] = hi, lo

    def source_z(k):
        return (zh + 4 - STEPS[k]) % 4

    def pass_on(k):
        block = x.at[source_z(k), c, y]
        arrived(block, az_r.at[k - 1])
        for i in (0, 2, 1):
            send(block, block, ay_s.at[k, i], ay_r.at[k, i], y_peers[i])

    def forward(k):
        zz = source_z(k)
        for i in (0, 2, 1):
            arrived(x.at[zz, c, (y - i - 1 + 4) % 4], ay_r.at[k, i])
        send(x.at[zz, c], x.at[zz, c], as_s.at[k], as_r.at[k], sibling)

    lane = lax.broadcasted_iota(jnp.int32, (64, 128), 1)

    def project(k):
        zz = source_z(k)
        arrived(x.at[zz, 1 - c], as_r.at[k])
        rows = pl.ds(pl.multiple_of(zz * 64, 64), 64)
        v = x[zz].reshape(64, XW)
        mixed = v[:, 1280:]
        th, tl = split(jnp.concatenate([v[:, :640], jnp.where(lane < 32, mixed, 0.0)], axis=1))
        gh, gl = split(jnp.concatenate([v[:, 640:1280], jnp.where(lane < 32, pltpu.roll(mixed, 96, 1), 0.0)], axis=1))
        xt_h[rows, :], xt_l[rows, :] = th, tl
        xg_h[rows, :], xg_l[rows, :] = gh, gl
        both = jnp.concatenate([th, tl], axis=0)
        gu = dot(both, wgu_h[...], 1, 0)
        gu = gu[:64] + gu[64:] + dot(th, wgu_l[...], 1, 0)
        both = jnp.concatenate([gh, gl], axis=0)
        hid = dot(both, wd_h[...], 1, 1)
        hid = hid[:64] + hid[64:] + dot(gh, wd_l[...], 1, 1)
        part[k] = pack3(gu[:, :FP], gu[:, FP:], hid).reshape(8, 8, AW)
        for i in range(7):
            send(part.at[k, (wa + i + 1) % 8], part_in.at[k, i], b_s.at[k, i], b_r.at[k, i], w_peers[i])

    def activate(k):
        zz = source_z(k)
        total = part[k, wa]
        for i in range(7):
            arrived(part_in.at[k, i], b_r.at[k, i])
            total = total + part_in[k, i]
        gate, up, gh = unpack3(total)
        acts[zz, wa] = pack3(*derivs(gate, up, gh))
        mine = acts.at[zz, wa]
        for i in range(7):
            send(mine, mine, c_s.at[k, i], c_r.at[k, i], w_peers[i])

    def back(k):
        zz = source_z(k)
        for i in range(7):
            arrived(acts.at[zz, (wa - i - 1 + 8) % 8], c_r.at[k, i])
        rows = pl.ds(pl.multiple_of(zz * 64, 64), 64)
        gga, gua, hid = unpack3(acts[zz].reshape(64, AW))
        ah, al = split(jnp.concatenate([gga, gua], axis=1))
        hh, hl = split(hid)
        a_h[rows, :DP], a_l[rows, :DP] = ah, al
        a_h[rows, DP:], a_l[rows, DP:] = hh, hl
        both = jnp.concatenate([ah, al], axis=0)
        gt = dot(both, wgu_h[...], 1, 1)
        gt = gt[:64] + gt[64:] + dot(ah, wgu_l[...], 1, 1)
        gb[k] = gt.reshape(2, 4, 8, DP)
        send(gb.at[k, 1 - c], gb_in.at[k], d1_s.at[k], d1_r.at[k], sibling)

    def home(k):
        arrived(gb_in.at[k], d1_r.at[k])
        q[k] = gb[k, c] + gb_in[k]
        for i in (1, 0, 2):
            send(q.at[k, (y + i + 1) % 4], q_in.at[k, i], d2_s.at[k, i], d2_r.at[k, i], y_peers[i])

    def collect(k):
        total = q[k, y]
        for i in range(3):
            arrived(q_in.at[k, i], d2_r.at[k, i])
            total = total + q_in[k, i]
        r[k] = total
        if k:
            send(r.at[k], r_in.at[k - 1], d3_s.at[k - 1], d3_r.at[k - 1], dev(wa, y, source_z(k), c))

    def grad(lh, ll, rh, rl):
        return dot(lh, rh, 0, 0) + dot(lh, rl, 0, 0) + dot(ll, rh, 0, 0)

    forward(0)
    pass_on(1)
    pass_on(3)
    pass_on(2)
    project(0)
    forward(1)
    forward(3)
    project(1)
    project(3)
    forward(2)
    project(2)
    activate(1)
    activate(3)
    activate(2)
    activate(0)
    back(1)
    home(1)
    back(3)
    home(3)
    back(2)
    collect(1)
    home(2)
    collect(3)
    back(0)
    collect(2)
    home(0)
    gg = grad(xt_h[...], xt_l[...], a_h[:, :FP], a_l[:, :FP])
    o_g[...] = gg[:DL, :FL]
    gg = grad(xt_h[...], xt_l[...], a_h[:, FP:DP], a_l[:, FP:DP])
    o_u[...] = gg[:DL, :FL]
    collect(0)
    gg = grad(a_h[:, DP:], a_l[:, DP:], xg_h[...], xg_l[...])
    o_d[...] = gg[:FL, :DL]

    total = r[0]
    for i in range(3):
        arrived(r_in.at[i], d3_r.at[i])
        total = total + r_in[i]
    o_tok[...] = total[:, :DL]
    for cp in sends:
        cp.wait_send()


def write_out(*refs):
    sem = refs[-1]
    copies = [pltpu.make_async_copy(refs[i], refs[4 + i], sem.at[i]) for i in range(4)]
    for cp in copies:
        cp.start()
    for cp in copies:
        cp.wait()


def per_device(tokens, grad_out, gate_weight, up_weight, down_weight):
    vm, anym = pl.BlockSpec(memory_space=pltpu.VMEM), pl.BlockSpec(memory_space=pltpu.MemorySpace.HBM)
    dma = pltpu.SemaphoreType.DMA
    v = pltpu.VMEM
    shapes = tuple(jax.ShapeDtypeStruct(s, F32) for s in ((8, DL), (DL, FL), (DL, FL), (FL, DL)))
    hbm = pltpu.MemorySpace.HBM
    tokens, grad_out, gate_weight, up_weight, down_weight = (
        pltpu.with_memory_space_constraint(a, hbm) for a in (tokens, grad_out, gate_weight, up_weight, down_weight)
    )
    results = pl.pallas_call(
        kernel,
        out_shape=shapes,
        in_specs=[vm, vm, anym, anym, anym],
        out_specs=(vm,) * 4,
        scratch_shapes=[
            v((DL, FL), F32), v((DL, FL), F32), v((FL, DL), F32),
            v((DP, DP), BF16), v((DP, DP), BF16), v((FP, DP), BF16), v((FP, DP), BF16),
            v((4, 2, 4, 8, XW), F32),
            v((256, DP), BF16), v((256, DP), BF16), v((256, DP), BF16), v((256, DP), BF16),
            v((4, 8, 8, AW), F32), v((4, 7, 8, AW), F32), v((4, 8, 8, AW), F32),
            v((256, DP + FP), BF16), v((256, DP + FP), BF16),
            v((4, 2, 4, 8, DP), F32), v((4, 4, 8, DP), F32), v((4, 4, 8, DP), F32), v((4, 3, 8, DP), F32),
            v((4, 8, DP), F32), v((3, 8, DP), F32),
            dma((3,)), dma((3,)), dma((3,)), dma((4, 3)), dma((4, 3)), dma((4,)), dma((4,)),
            dma((4, 7)), dma((4, 7)), dma((4, 7)), dma((4, 7)),
            dma((4,)), dma((4,)), dma((4, 3)), dma((4, 3)), dma((3,)), dma((3,)),
        ],
        compiler_params=pltpu.CompilerParams(collective_id=0, has_side_effects=True, vmem_limit_bytes=40 * 2**20),
        name="feed_forward_backward",
    )(tokens, grad_out, gate_weight, up_weight, down_weight)
    return pl.pallas_call(
        write_out,
        out_shape=shapes,
        in_specs=[anym] * 4,
        out_specs=(anym,) * 4,
        scratch_shapes=[dma((4,))],
        compiler_params=pltpu.CompilerParams(vmem_limit_bytes=2**20),
        name="write_out",
    )(*results)


def solution(mesh):
    placed = (P("ha", "wa"), P("ha", "wa"), P("wa", "ha"), P("wa", "ha"), P("ha", "wa"))
    return jax.shard_map(
        per_device,
        mesh=mesh,
        in_specs=placed,
        out_specs=(P("ha", "wa"), P("wa", "ha"), P("wa", "ha"), P("ha", "wa")),
        check_vma=False,
    )
```

```python
import jax
import jax.numpy as jnp
from jax import lax
from jax.experimental import pallas as pl
from jax.experimental.pallas import tpu as pltpu
from jax.sharding import PartitionSpec as P

MESH = pl.DeviceIdType.MESH
F32, BF16 = jnp.float32, jnp.bfloat16
DL, FL = 672, 336
DP, FP = 768, 384
XW, AW = 1408, 1024
STEPS = (0, 1, 2, 3)
STAGED = (0,)
FAR_FIRST = (1, 0, 2)


def split(v):
    hi = v.astype(BF16)
    return hi, (v - hi.astype(F32)).astype(BF16)


def dot(a, b, ad, bd):
    return lax.dot_general(a, b, (((ad,), (bd,)), ((), ())), preferred_element_type=F32)


def pack3(a, b, c):
    rows = a.shape[0]
    return jnp.concatenate([a[:, :FL], b[:, :FL], c[:, :FL], jnp.zeros((rows, AW - 3 * FL), F32)], axis=1)


def unpack3(p):
    pad = jnp.zeros((p.shape[0], FP - FL), F32)
    return [jnp.concatenate([p[:, i * FL : (i + 1) * FL], pad], axis=1) for i in range(3)]


def derivs(gate, up, grad_hidden):
    sig = 1.0 / (1.0 + jnp.exp(-gate))
    hidden = gate * sig * up
    grad_up_act = grad_hidden * gate * sig
    grad_gate_act = grad_hidden * up * sig * (1.0 + gate * (1.0 - sig))
    return grad_gate_act, grad_up_act, hidden


def kernel(
    tok_hbm, gro_hbm, wg_hbm, wu_hbm, wd_hbm,
    o_tok, o_g, o_u, o_d,
    tok, gro, wg, wu, wd, wgu_h, wgu_l, wd_h, wd_l,
    x, xt_h, xt_l, xg_h, xg_l,
    part, near, far, right, right_in, right2_in, acts, a_h, a_l,
    gb, gb_in, q, q_in, r, r_in,
    w_sem, az_s, az_r, ay_s, ay_r, as_s, as_r,
    b_s, b_r, c_s, c_r, d1_s, d1_r, d2_s, d2_r, d3_s, d3_r,
):
    wa, ha = lax.axis_index("wa"), lax.axis_index("ha")
    y, zh, c = ha // 8, (ha // 2) % 4, ha % 2

    def dev(w, yy, zz, cc):
        return (w, yy * 8 + zz * 2 + cc)

    sibling = dev(wa, y, zh, 1 - c)
    z_peers = [dev(wa, y, (zh + i) % 4, c) for i in (1, 2, 3)]
    y_peers = [dev(wa, (y + s) % 4, zh, c) for s in STEPS[1:]]
    zl, xx = wa // 4, wa % 4
    partner = dev((1 - zl) * 4 + xx, y, zh, c)
    x_peers = [dev(zl * 4 + (xx + i) % 4, y, zh, c) for i in (1, 2, 3)]
    cross = [((xx + i) % 4, dev((1 - zl) * 4 + (xx + i) % 4, y, zh, c)) for i in (1, 2, 3)]

    first = [
        pltpu.make_async_copy(tok_hbm, tok, w_sem.at[3]),
        pltpu.make_async_copy(gro_hbm, gro, w_sem.at[4]),
    ]
    loads = [
        pltpu.make_async_copy(wg_hbm, wg, w_sem.at[0]),
        pltpu.make_async_copy(wu_hbm, wu, w_sem.at[1]),
        pltpu.make_async_copy(wd_hbm, wd, w_sem.at[2]),
    ]
    for cp in first:
        cp.start()

    barrier = pltpu.get_barrier_semaphore()
    for d in [sibling, *z_peers, *y_peers, partner, *x_peers, *[d for _, d in cross]]:
        pl.semaphore_signal(barrier, inc=1, device_id=d, device_id_type=MESH)
    first[0].wait()
    first[1].wait()
    t, g = tok[...], gro[...]
    x[zh, c, y] = jnp.concatenate([t[:, :640], g[:, :640], t[:, 640:], g[:, 640:], jnp.zeros((8, 64), F32)], axis=1)
    for cp in loads:
        cp.start()
    pl.semaphore_wait(barrier, 14)

    sends = []

    def send(src, dst, ss, rs, d):
        cp = pltpu.make_async_remote_copy(src_ref=src, dst_ref=dst, send_sem=ss, recv_sem=rs, device_id=d, device_id_type=MESH)
        cp.start()
        sends.append(cp)

    def arrived(ref, sem):
        pltpu.make_async_copy(ref, ref, sem).wait()

    own = x.at[zh, c, y]
    for i in FAR_FIRST:
        send(own, own, ay_s.at[0, i], ay_r.at[0, i], y_peers[i])
    for i in (0, 2, 1):
        send(own, own, az_s.at[i], az_r.at[i], z_peers[i])

    wgu_h[DL:, :] = jnp.zeros((DP - DL, DP), BF16)
    wgu_l[DL:, :] = jnp.zeros((DP - DL, DP), BF16)
    wd_h[FL:, :] = jnp.zeros((FP - FL, DP), BF16)
    wd_l[FL:, :] = jnp.zeros((FP - FL, DP), BF16)
    loads[0].wait()
    loads[1].wait()

    @pl.loop(0, 7)
    def _(i):
        rows = pl.ds(pl.multiple_of(i * 96, 96), 96)
        pad = jnp.zeros((96, FP - FL), F32)
        hi, lo = split(jnp.concatenate([wg[rows, :], pad], axis=1))
        wgu_h[rows, :FP], wgu_l[rows, :FP] = hi, lo
        hi, lo = split(jnp.concatenate([wu[rows, :], pad], axis=1))
        wgu_h[rows, FP:], wgu_l[rows, FP:] = hi, lo

    loads[2].wait()

    @pl.loop(0, 7)
    def _(i):
        rows = pl.ds(pl.multiple_of(i * 48, 48), 48)
        hi, lo = split(jnp.concatenate([wd[rows, :], jnp.zeros((48, DP - DL), F32)], axis=1))
        wd_h[rows, :], wd_l[rows, :] = hi, lo

    def source_z(k):
        return (zh + 4 - STEPS[k]) % 4

    def pass_on(k):
        block = x.at[source_z(k), c, y]
        arrived(block, az_r.at[k - 1])
        for i in FAR_FIRST:
            send(block, block, ay_s.at[k, i], ay_r.at[k, i], y_peers[i])

    def forward(k):
        zz = source_z(k)
        for i in (0, 2, 1):
            arrived(x.at[zz, c, (y - i - 1 + 4) % 4], ay_r.at[k, i])
        send(x.at[zz, c], x.at[zz, c], as_s.at[k], as_r.at[k], sibling)

    lane = lax.broadcasted_iota(jnp.int32, (64, 128), 1)

    def project(k):
        zz = source_z(k)
        arrived(x.at[zz, 1 - c], as_r.at[k])
        rows = pl.ds(pl.multiple_of(zz * 64, 64), 64)
        v = x[zz].reshape(64, XW)
        mixed = v[:, 1280:]
        th, tl = split(jnp.concatenate([v[:, :640], jnp.where(lane < 32, mixed, 0.0)], axis=1))
        gh, gl = split(jnp.concatenate([v[:, 640:1280], jnp.where(lane < 32, pltpu.roll(mixed, 96, 1), 0.0)], axis=1))
        xt_h[rows, :], xt_l[rows, :] = th, tl
        xg_h[rows, :], xg_l[rows, :] = gh, gl
        both = jnp.concatenate([th, tl], axis=0)
        gu = dot(both, wgu_h[...], 1, 0)
        gu = gu[:64] + gu[64:] + dot(th, wgu_l[...], 1, 0)
        both = jnp.concatenate([gh, gl], axis=0)
        hid = dot(both, wd_h[...], 1, 1)
        hid = hid[:64] + hid[64:] + dot(gh, wd_l[...], 1, 1)
        part[k] = pack3(gu[:, :FP], gu[:, FP:], hid).reshape(4, 2, 8, AW)
        if k not in STAGED:
            for i in FAR_FIRST:
                send(part.at[k, cross[i][0], 1 - zl], far.at[k, i], b_s.at[k, 4 + i], b_r.at[k, 4 + i], cross[i][1])
            for i in FAR_FIRST:
                send(part.at[k, (xx + i + 1) % 4, zl], near.at[k, i], b_s.at[k, i], b_r.at[k, i], x_peers[i])
            send(part.at[k, xx, 1 - zl], far.at[k, 3], b_s.at[k, 3], b_r.at[k, 3], partner)
        else:
            for i in range(3):
                send(part.at[k, (xx + i + 1) % 4], right_in.at[k, i], b_s.at[k, i], b_r.at[k, i], x_peers[i])

    def reduce(k):
        total = part[k, xx]
        for i in range(3):
            arrived(right_in.at[k, i], b_r.at[k, i])
            total = total + right_in[k, i]
        right[k] = total
        send(right.at[k, 1 - zl], right2_in.at[k], b_s.at[k, 7], b_r.at[k, 7], partner)

    def activate(k):
        zz = source_z(k)
        if k not in STAGED:
            total = part[k, xx, zl]
            for i in range(3):
                arrived(near.at[k, i], b_r.at[k, i])
                total = total + near[k, i]
            for i in (3, 0, 1, 2):
                arrived(far.at[k, i], b_r.at[k, 3 if i == 3 else 4 + i])
                total = total + far[k, i]
        else:
            arrived(right2_in.at[k], b_r.at[k, 7])
            total = right[k, zl] + right2_in[k]
        gate, up, gh = unpack3(total)
        acts[zz, xx, zl] = pack3(*derivs(gate, up, gh))
        mine = acts.at[zz, xx, zl]
        for i in FAR_FIRST:
            send(mine, mine, c_s.at[k, 4 + i], c_r.at[k, 4 + i], cross[i][1])
        for i in FAR_FIRST:
            send(mine, mine, c_s.at[k, i], c_r.at[k, i], x_peers[i])
        send(mine, mine, c_s.at[k, 3], c_r.at[k, 3], partner)

    def back(k):
        zz = source_z(k)
        for i in range(3):
            x2 = (xx - i - 1 + 4) % 4
            arrived(acts.at[zz, x2, zl], c_r.at[k, i])
            arrived(acts.at[zz, x2, 1 - zl], c_r.at[k, 4 + i])
        arrived(acts.at[zz, xx, 1 - zl], c_r.at[k, 3])
        rows = pl.ds(pl.multiple_of(zz * 64, 64), 64)
        gga, gua, hid = unpack3(acts[zz].reshape(64, AW))
        ah, al = split(jnp.concatenate([gga, gua], axis=1))
        hh, hl = split(hid)
        a_h[rows, :DP], a_l[rows, :DP] = ah, al
        a_h[rows, DP:], a_l[rows, DP:] = hh, hl
        both = jnp.concatenate([ah, al], axis=0)
        gt = dot(both, wgu_h[...], 1, 1)
        gt = gt[:64] + gt[64:] + dot(ah, wgu_l[...], 1, 1)
        gb[k] = gt.reshape(2, 4, 8, DP)
        send(gb.at[k, 1 - c], gb_in.at[k], d1_s.at[k], d1_r.at[k], sibling)

    def home(k):
        arrived(gb_in.at[k], d1_r.at[k])
        q[k] = gb[k, c] + gb_in[k]
        for i in (1, 0, 2):
            send(q.at[k, (y + i + 1) % 4], q_in.at[k, i], d2_s.at[k, i], d2_r.at[k, i], y_peers[i])

    def collect(k):
        total = q[k, y]
        for i in range(3):
            arrived(q_in.at[k, i], d2_r.at[k, i])
            total = total + q_in[k, i]
        r[k] = total
        if k:
            send(r.at[k], r_in.at[k - 1], d3_s.at[k - 1], d3_r.at[k - 1], dev(wa, y, source_z(k), c))

    def grad(lh, ll, rh, rl):
        return dot(lh, rh, 0, 0) + dot(lh, rl, 0, 0) + dot(ll, rh, 0, 0)

    forward(0)
    pass_on(1)
    pass_on(3)
    pass_on(2)
    project(0)
    forward(1)
    forward(3)
    project(1)
    project(3)
    forward(2)
    project(2)
    reduce(0)
    activate(1)
    activate(2)
    activate(3)
    activate(0)
    back(1)
    home(1)
    back(2)
    home(2)
    collect(1)
    back(3)
    home(3)
    collect(2)
    back(0)
    home(0)
    collect(3)
    gg = grad(xt_h[...], xt_l[...], a_h[:, :FP], a_l[:, :FP])
    o_g[...] = gg[:DL, :FL]
    gg = grad(xt_h[...], xt_l[...], a_h[:, FP:DP], a_l[:, FP:DP])
    o_u[...] = gg[:DL, :FL]
    collect(0)
    gg = grad(a_h[:, DP:], a_l[:, DP:], xg_h[...], xg_l[...])
    o_d[...] = gg[:FL, :DL]

    total = r[0]
    for i in range(3):
        arrived(r_in.at[i], d3_r.at[i])
        total = total + r_in[i]
    o_tok[...] = total[:, :DL]
    for cp in sends:
        cp.wait_send()


def write_out(*refs):
    sem = refs[-1]
    copies = [pltpu.make_async_copy(refs[i], refs[4 + i], sem.at[i]) for i in range(4)]
    for cp in copies:
        cp.start()
    for cp in copies:
        cp.wait()


def per_device(tokens, grad_out, gate_weight, up_weight, down_weight):
    vm, anym = pl.BlockSpec(memory_space=pltpu.VMEM), pl.BlockSpec(memory_space=pltpu.MemorySpace.HBM)
    dma = pltpu.SemaphoreType.DMA
    v = pltpu.VMEM
    shapes = tuple(jax.ShapeDtypeStruct(s, F32) for s in ((8, DL), (DL, FL), (DL, FL), (FL, DL)))
    hbm = pltpu.MemorySpace.HBM
    tokens, grad_out, gate_weight, up_weight, down_weight = (
        pltpu.with_memory_space_constraint(a, hbm) for a in (tokens, grad_out, gate_weight, up_weight, down_weight)
    )
    results = pl.pallas_call(
        kernel,
        out_shape=shapes,
        in_specs=[anym] * 5,
        out_specs=(vm,) * 4,
        scratch_shapes=[
            v((8, DL), F32), v((8, DL), F32), v((DL, FL), F32), v((DL, FL), F32), v((FL, DL), F32),
            v((DP, DP), BF16), v((DP, DP), BF16), v((FP, DP), BF16), v((FP, DP), BF16),
            v((4, 2, 4, 8, XW), F32),
            v((256, DP), BF16), v((256, DP), BF16), v((256, DP), BF16), v((256, DP), BF16),
            v((4, 4, 2, 8, AW), F32), v((4, 3, 8, AW), F32), v((4, 4, 8, AW), F32),
            v((4, 2, 8, AW), F32), v((4, 3, 2, 8, AW), F32), v((4, 8, AW), F32),
            v((4, 4, 2, 8, AW), F32),
            v((256, DP + FP), BF16), v((256, DP + FP), BF16),
            v((4, 2, 4, 8, DP), F32), v((4, 4, 8, DP), F32), v((4, 4, 8, DP), F32), v((4, 3, 8, DP), F32),
            v((4, 8, DP), F32), v((3, 8, DP), F32),
            dma((5,)), dma((3,)), dma((3,)), dma((4, 3)), dma((4, 3)), dma((4,)), dma((4,)),
            dma((4, 8)), dma((4, 8)), dma((4, 8)), dma((4, 8)),
            dma((4,)), dma((4,)), dma((4, 3)), dma((4, 3)), dma((3,)), dma((3,)),
        ],
        compiler_params=pltpu.CompilerParams(collective_id=0, has_side_effects=True, vmem_limit_bytes=40 * 2**20),
        name="feed_forward_backward",
    )(tokens, grad_out, gate_weight, up_weight, down_weight)
    return pl.pallas_call(
        write_out,
        out_shape=shapes,
        in_specs=[anym] * 4,
        out_specs=(anym,) * 4,
        scratch_shapes=[dma((4,))],
        compiler_params=pltpu.CompilerParams(vmem_limit_bytes=2**20),
        name="write_out",
    )(*results)


def solution(mesh):
    placed = (P("ha", "wa"), P("ha", "wa"), P("wa", "ha"), P("wa", "ha"), P("ha", "wa"))
    return jax.shard_map(
        per_device,
        mesh=mesh,
        in_specs=placed,
        out_specs=(P("ha", "wa"), P("wa", "ha"), P("wa", "ha"), P("ha", "wa")),
        check_vma=False,
    )
```

```python
import jax
import jax.numpy as jnp
from jax import lax
from jax.experimental import pallas as pl
from jax.experimental.pallas import tpu as pltpu
from jax.sharding import PartitionSpec as P

MESH = pl.DeviceIdType.MESH
F32, BF16 = jnp.float32, jnp.bfloat16
DL, FL = 672, 336
DP, FP = 768, 384
XW, AW = 1408, 1024
STEPS = (0, 1, 2, 3)
STAGED = (0,)
FAR_FIRST = (1, 0, 2)


def split(v):
    hi = v.astype(BF16)
    return hi, (v - hi.astype(F32)).astype(BF16)


def dot(a, b, ad, bd):
    return lax.dot_general(a, b, (((ad,), (bd,)), ((), ())), preferred_element_type=F32)


def pack3(a, b, c):
    rows = a.shape[0]
    return jnp.concatenate([a[:, :FL], b[:, :FL], c[:, :FL], jnp.zeros((rows, AW - 3 * FL), F32)], axis=1)


def unpack3(p):
    pad = jnp.zeros((p.shape[0], FP - FL), F32)
    return [jnp.concatenate([p[:, i * FL : (i + 1) * FL], pad], axis=1) for i in range(3)]


def derivs(gate, up, grad_hidden):
    sig = 1.0 / (1.0 + jnp.exp(-gate))
    hidden = gate * sig * up
    grad_up_act = grad_hidden * gate * sig
    grad_gate_act = grad_hidden * up * sig * (1.0 + gate * (1.0 - sig))
    return grad_gate_act, grad_up_act, hidden


def kernel(
    tok_hbm, gro_hbm, wg_hbm, wu_hbm, wd_hbm,
    o_tok, o_g, o_u, o_d,
    tok, gro, wg, wu, wd, wgu_h, wgu_l, wd_h, wd_l,
    x, xt_h, xt_l, xg_h, xg_l,
    part, near, far, right, right_in, right2_in, acts, a_h, a_l,
    gb, gb_in, q, q_in, r, r_in,
    w_sem, az_s, az_r, ay_s, ay_r, as_s, as_r,
    b_s, b_r, c_s, c_r, d1_s, d1_r, d2_s, d2_r, d3_s, d3_r,
):
    wa, ha = lax.axis_index("wa"), lax.axis_index("ha")
    y, zh, c = ha // 8, (ha // 2) % 4, ha % 2

    def dev(w, yy, zz, cc):
        return (w, yy * 8 + zz * 2 + cc)

    sibling = dev(wa, y, zh, 1 - c)
    z_peers = [dev(wa, y, (zh + i) % 4, c) for i in (1, 2, 3)]
    y_peers = [dev(wa, (y + s) % 4, zh, c) for s in STEPS[1:]]
    zl, xx = wa // 4, wa % 4
    partner = dev((1 - zl) * 4 + xx, y, zh, c)
    x_peers = [dev(zl * 4 + (xx + i) % 4, y, zh, c) for i in (1, 2, 3)]
    cross = [((xx + i) % 4, dev((1 - zl) * 4 + (xx + i) % 4, y, zh, c)) for i in (1, 2, 3)]

    first = [
        pltpu.make_async_copy(tok_hbm, tok, w_sem.at[3]),
        pltpu.make_async_copy(gro_hbm, gro, w_sem.at[4]),
    ]
    loads = [
        pltpu.make_async_copy(wg_hbm, wg, w_sem.at[0]),
        pltpu.make_async_copy(wu_hbm, wu, w_sem.at[1]),
        pltpu.make_async_copy(wd_hbm, wd, w_sem.at[2]),
    ]
    for cp in first:
        cp.start()

    barrier = pltpu.get_barrier_semaphore()
    for d in [sibling, *z_peers, *y_peers, partner, *x_peers, *[d for _, d in cross]]:
        pl.semaphore_signal(barrier, inc=1, device_id=d, device_id_type=MESH)
    first[0].wait()
    first[1].wait()
    t, g = tok[...], gro[...]
    x[zh, c, y] = jnp.concatenate([t[:, :640], g[:, :640], t[:, 640:], g[:, 640:], jnp.zeros((8, 64), F32)], axis=1)
    for cp in loads:
        cp.start()
    pl.semaphore_wait(barrier, 14)

    sends = []

    def send(src, dst, ss, rs, d):
        cp = pltpu.make_async_remote_copy(src_ref=src, dst_ref=dst, send_sem=ss, recv_sem=rs, device_id=d, device_id_type=MESH)
        cp.start()
        sends.append(cp)

    def arrived(ref, sem):
        pltpu.make_async_copy(ref, ref, sem).wait()

    own = x.at[zh, c, y]
    for i in FAR_FIRST:
        send(own, own, ay_s.at[0, i], ay_r.at[0, i], y_peers[i])
    for i in (0, 2, 1):
        send(own, own, az_s.at[i], az_r.at[i], z_peers[i])

    wgu_h[DL:, :] = jnp.zeros((DP - DL, DP), BF16)
    wgu_l[DL:, :] = jnp.zeros((DP - DL, DP), BF16)
    wd_h[FL:, :] = jnp.zeros((FP - FL, DP), BF16)
    wd_l[FL:, :] = jnp.zeros((FP - FL, DP), BF16)
    loads[0].wait()
    loads[1].wait()

    @pl.loop(0, 7)
    def _(i):
        rows = pl.ds(pl.multiple_of(i * 96, 96), 96)
        pad = jnp.zeros((96, FP - FL), F32)
        hi, lo = split(jnp.concatenate([wg[rows, :], pad], axis=1))
        wgu_h[rows, :FP], wgu_l[rows, :FP] = hi, lo
        hi, lo = split(jnp.concatenate([wu[rows, :], pad], axis=1))
        wgu_h[rows, FP:], wgu_l[rows, FP:] = hi, lo

    loads[2].wait()

    @pl.loop(0, 7)
    def _(i):
        rows = pl.ds(pl.multiple_of(i * 48, 48), 48)
        hi, lo = split(jnp.concatenate([wd[rows, :], jnp.zeros((48, DP - DL), F32)], axis=1))
        wd_h[rows, :], wd_l[rows, :] = hi, lo

    def source_z(k):
        return (zh + 4 - STEPS[k]) % 4

    def pass_on(k):
        block = x.at[source_z(k), c, y]
        arrived(block, az_r.at[k - 1])
        for i in FAR_FIRST:
            send(block, block, ay_s.at[k, i], ay_r.at[k, i], y_peers[i])

    def forward(k):
        zz = source_z(k)
        for i in (0, 2, 1):
            arrived(x.at[zz, c, (y - i - 1 + 4) % 4], ay_r.at[k, i])
        send(x.at[zz, c], x.at[zz, c], as_s.at[k], as_r.at[k], sibling)

    lane = lax.broadcasted_iota(jnp.int32, (64, 128), 1)

    def project(k):
        zz = source_z(k)
        arrived(x.at[zz, 1 - c], as_r.at[k])
        rows = pl.ds(pl.multiple_of(zz * 64, 64), 64)
        v = x[zz].reshape(64, XW)
        mixed = v[:, 1280:]
        th, tl = split(jnp.concatenate([v[:, :640], jnp.where(lane < 32, mixed, 0.0)], axis=1))
        gh, gl = split(jnp.concatenate([v[:, 640:1280], jnp.where(lane < 32, pltpu.roll(mixed, 96, 1), 0.0)], axis=1))
        xt_h[rows, :], xt_l[rows, :] = th, tl
        xg_h[rows, :], xg_l[rows, :] = gh, gl
        both = jnp.concatenate([th, tl], axis=0)
        gu = dot(both, wgu_h[...], 1, 0)
        gu = gu[:64] + gu[64:] + dot(th, wgu_l[...], 1, 0)
        both = jnp.concatenate([gh, gl], axis=0)
        hid = dot(both, wd_h[...], 1, 1)
        hid = hid[:64] + hid[64:] + dot(gh, wd_l[...], 1, 1)
        part[k] = pack3(gu[:, :FP], gu[:, FP:], hid).reshape(4, 2, 8, AW)
        if k not in STAGED:
            for i in FAR_FIRST:
                send(part.at[k, cross[i][0], 1 - zl], far.at[k, i], b_s.at[k, 4 + i], b_r.at[k, 4 + i], cross[i][1])
            for i in FAR_FIRST:
                send(part.at[k, (xx + i + 1) % 4, zl], near.at[k, i], b_s.at[k, i], b_r.at[k, i], x_peers[i])
            send(part.at[k, xx, 1 - zl], far.at[k, 3], b_s.at[k, 3], b_r.at[k, 3], partner)
        else:
            for i in range(3):
                send(part.at[k, (xx + i + 1) % 4], right_in.at[k, i], b_s.at[k, i], b_r.at[k, i], x_peers[i])

    def reduce(k):
        total = part[k, xx]
        for i in range(3):
            arrived(right_in.at[k, i], b_r.at[k, i])
            total = total + right_in[k, i]
        right[k] = total
        send(right.at[k, 1 - zl], right2_in.at[k], b_s.at[k, 7], b_r.at[k, 7], partner)

    def activate(k):
        zz = source_z(k)
        if k not in STAGED:
            total = part[k, xx, zl]
            for i in range(3):
                arrived(near.at[k, i], b_r.at[k, i])
                total = total + near[k, i]
            for i in (3, 0, 1, 2):
                arrived(far.at[k, i], b_r.at[k, 3 if i == 3 else 4 + i])
                total = total + far[k, i]
        else:
            arrived(right2_in.at[k], b_r.at[k, 7])
            total = right[k, zl] + right2_in[k]
        gate, up, gh = unpack3(total)
        acts[zz, xx, zl] = pack3(*derivs(gate, up, gh))
        mine = acts.at[zz, xx, zl]
        for i in FAR_FIRST:
            send(mine, mine, c_s.at[k, 4 + i], c_r.at[k, 4 + i], cross[i][1])
        for i in FAR_FIRST:
            send(mine, mine, c_s.at[k, i], c_r.at[k, i], x_peers[i])
        send(mine, mine, c_s.at[k, 3], c_r.at[k, 3], partner)

    def back(k):
        zz = source_z(k)
        for i in range(3):
            x2 = (xx - i - 1 + 4) % 4
            arrived(acts.at[zz, x2, zl], c_r.at[k, i])
            arrived(acts.at[zz, x2, 1 - zl], c_r.at[k, 4 + i])
        arrived(acts.at[zz, xx, 1 - zl], c_r.at[k, 3])
        rows = pl.ds(pl.multiple_of(zz * 64, 64), 64)
        gga, gua, hid = unpack3(acts[zz].reshape(64, AW))
        ah, al = split(jnp.concatenate([gga, gua], axis=1))
        hh, hl = split(hid)
        a_h[rows, :DP], a_l[rows, :DP] = ah, al
        a_h[rows, DP:], a_l[rows, DP:] = hh, hl
        both = jnp.concatenate([ah, al], axis=0)
        gt = dot(both, wgu_h[...], 1, 1)
        gt = gt[:64] + gt[64:] + dot(ah, wgu_l[...], 1, 1)
        gb[k] = gt.reshape(2, 4, 8, DP)
        send(gb.at[k, 1 - c], gb_in.at[k], d1_s.at[k], d1_r.at[k], sibling)

    def home(k):
        arrived(gb_in.at[k], d1_r.at[k])
        q[k] = gb[k, c] + gb_in[k]
        for i in (1, 0, 2):
            send(q.at[k, (y + i + 1) % 4], q_in.at[k, i], d2_s.at[k, i], d2_r.at[k, i], y_peers[i])

    def collect(k):
        total = q[k, y]
        for i in range(3):
            arrived(q_in.at[k, i], d2_r.at[k, i])
            total = total + q_in[k, i]
        r[k] = total
        if k:
            send(r.at[k], r_in.at[k - 1], d3_s.at[k - 1], d3_r.at[k - 1], dev(wa, y, source_z(k), c))

    def grad(lh, ll, rh, rl):
        return dot(lh, rh, 0, 0) + dot(lh, rl, 0, 0) + dot(ll, rh, 0, 0)

    forward(0)
    pass_on(1)
    pass_on(3)
    pass_on(2)
    project(0)
    forward(1)
    forward(3)
    project(1)
    project(3)
    forward(2)
    project(2)
    reduce(0)
    activate(1)
    activate(2)
    activate(3)
    activate(0)
    back(1)
    home(1)
    back(2)
    home(2)
    collect(1)
    back(3)
    home(3)
    collect(2)
    back(0)
    home(0)
    collect(3)
    gg = grad(xt_h[...], xt_l[...], a_h[:, :FP], a_l[:, :FP])
    o_g[...] = gg[:DL, :FL]
    gg = grad(xt_h[...], xt_l[...], a_h[:, FP:DP], a_l[:, FP:DP])
    o_u[...] = gg[:DL, :FL]
    collect(0)
    gg = grad(a_h[:, DP:], a_l[:, DP:], xg_h[...], xg_l[...])
    o_d[...] = gg[:FL, :DL]

    for cp in sends:
        cp.wait_send()
    total = r[0]
    for i in range(3):
        arrived(r_in.at[i], d3_r.at[i])
        total = total + r_in[i]
    o_tok[...] = total[:, :DL]


def write_out(*refs):
    sem = refs[-1]
    copies = [pltpu.make_async_copy(refs[i], refs[4 + i], sem.at[i]) for i in range(4)]
    for cp in copies:
        cp.start()
    for cp in copies:
        cp.wait()


def per_device(tokens, grad_out, gate_weight, up_weight, down_weight):
    vm, anym = pl.BlockSpec(memory_space=pltpu.VMEM), pl.BlockSpec(memory_space=pltpu.MemorySpace.HBM)
    dma = pltpu.SemaphoreType.DMA
    v = pltpu.VMEM
    shapes = tuple(jax.ShapeDtypeStruct(s, F32) for s in ((8, DL), (DL, FL), (DL, FL), (FL, DL)))
    hbm = pltpu.MemorySpace.HBM
    tokens, grad_out, gate_weight, up_weight, down_weight = (
        pltpu.with_memory_space_constraint(a, hbm) for a in (tokens, grad_out, gate_weight, up_weight, down_weight)
    )
    results = pl.pallas_call(
        kernel,
        out_shape=shapes,
        in_specs=[anym] * 5,
        out_specs=(vm,) * 4,
        scratch_shapes=[
            v((8, DL), F32), v((8, DL), F32), v((DL, FL), F32), v((DL, FL), F32), v((FL, DL), F32),
            v((DP, DP), BF16), v((DP, DP), BF16), v((FP, DP), BF16), v((FP, DP), BF16),
            v((4, 2, 4, 8, XW), F32),
            v((256, DP), BF16), v((256, DP), BF16), v((256, DP), BF16), v((256, DP), BF16),
            v((4, 4, 2, 8, AW), F32), v((4, 3, 8, AW), F32), v((4, 4, 8, AW), F32),
            v((4, 2, 8, AW), F32), v((4, 3, 2, 8, AW), F32), v((4, 8, AW), F32),
            v((4, 4, 2, 8, AW), F32),
            v((256, DP + FP), BF16), v((256, DP + FP), BF16),
            v((4, 2, 4, 8, DP), F32), v((4, 4, 8, DP), F32), v((4, 4, 8, DP), F32), v((4, 3, 8, DP), F32),
            v((4, 8, DP), F32), v((3, 8, DP), F32),
            dma((5,)), dma((3,)), dma((3,)), dma((4, 3)), dma((4, 3)), dma((4,)), dma((4,)),
            dma((4, 8)), dma((4, 8)), dma((4, 8)), dma((4, 8)),
            dma((4,)), dma((4,)), dma((4, 3)), dma((4, 3)), dma((3,)), dma((3,)),
        ],
        compiler_params=pltpu.CompilerParams(collective_id=0, has_side_effects=True, vmem_limit_bytes=40 * 2**20),
        name="feed_forward_backward",
    )(tokens, grad_out, gate_weight, up_weight, down_weight)
    return pl.pallas_call(
        write_out,
        out_shape=shapes,
        in_specs=[anym] * 4,
        out_specs=(anym,) * 4,
        scratch_shapes=[dma((4,))],
        compiler_params=pltpu.CompilerParams(vmem_limit_bytes=2**20),
        name="write_out",
    )(*results)


def solution(mesh):
    placed = (P("ha", "wa"), P("ha", "wa"), P("wa", "ha"), P("wa", "ha"), P("ha", "wa"))
    return jax.shard_map(
        per_device,
        mesh=mesh,
        in_specs=placed,
        out_specs=(P("ha", "wa"), P("wa", "ha"), P("wa", "ha"), P("ha", "wa")),
        check_vma=False,
    )
```
